32 devices in a mesh: rep: 4 (over y, x), shard: 8 (over z, core).
Axes of the slice: x: 2, y: 2, z: 4, core: 2. Of those that a mesh axis runs over, the one named last changes fastest.
Arguments:
- tokens: bfloat16 [32768, 768], P(('rep', 'shard')), may hold values from -6 to 6
- seg_ids: int32 [32768], P(('rep', 'shard')), may hold values from 0 to 95, never falling along the last dimension, each value on 1 to 1024 neighbouring positions
- norm_in_w: bfloat16 [768], P('shard'), may hold values from 0.5 to 1.5
- in_proj: bfloat16 [768, 3352], P('shard'), may hold values from -0.21875 to 0.21875
- conv_w: bfloat16 [4, 1792], P(None, 'shard'), may hold values from -3 to 3
- conv_b: bfloat16 [1792], P('shard'), may hold values from -1.796875 to 1.796875
- a_log: float32 [24], replicated, may hold values from 0 to 2.7
- skip_d: float32 [24], replicated, may hold values from 0.5 to 1.5
- dt_bias: float32 [24], replicated, may hold values from -6.5 to -2.5
- gnorm_w: bfloat16 [1536], P('shard'), may hold values from 0.5 to 1.5
- out_proj: bfloat16 [1536, 768], P('shard'), may hold values from -0.15625 to 0.15625
- cotangent: bfloat16 [32768, 768], P(('rep', 'shard')), may hold values from -6 to 6
Outputs:
- output: bfloat16 [32768, 768], P(('rep', 'shard'))
- grad_tokens: float32 [32768, 768], P(('rep', 'shard'))
- grad_norm_in: float32 [768], P('shard')
- grad_in_proj: float32 [768, 3352], P('shard')
- grad_conv_w: float32 [4, 1792], P(None, 'shard')
- grad_conv_b: float32 [1792], P('shard')
- grad_a_log: float32 [24], replicated
- grad_skip_d: float32 [24], replicated
- grad_dt_bias: float32 [24], replicated
- grad_gnorm: float32 [1536], P('shard')
- grad_out_proj: float32 [1536, 768], P('shard')
The draws below stay inside these ranges and needn't reach their ends.
Inputs may be any that keep to these rules, and one draw needn't show every extreme that they name: seg_ids never fall from one token to the next, and each segment has 1 to 1024 tokens.
All inputs are finite; a program needn't handle non-finite values.
Results may differ from the reference program's by a relative error of at most 0.011.
Values may be sent and summed in bfloat16 or wider, within the bound.
A program may use at most 192 MiB of HBM per device.

```python
import math
import jax
import jax.numpy as jnp
import numpy as np
from jax import lax

D = 768
DIN = 1536
NH = 24
HD = 64
NS = 128
DCONV = 4
BLOCK = 256
LENGTH = 1024
SEQS = 32
TOKENS = 32768
CONVDIM = 1792
DPROJ = 3352


def shard_levels(own_key, dims, split, smallest, largest):
    level, own = 1.0, jax.random.fold_in(own_key, 6)
    for dim, blocks in split:
        heights = jnp.exp(jax.random.uniform(jax.random.fold_in(own, dim), (blocks,), jnp.float32, smallest / len(split), largest / len(split)))
        level = level * jnp.repeat(heights, dims[dim] // blocks).reshape([-1 if axis == dim else 1 for axis in range(len(dims))])
    return level


def profile(count, total, bound, slope):
    portions = [(1 << 20) // math.isqrt(standing ** slope) + 1 for standing in range(2, count + 1)]
    rest, holding = total - bound - (count - 1), [1] * (count - 1)
    while rest > 0:
        candidates = [i for i in range(count - 1) if holding[i] < bound]
        whole, budget = sum([portions[i] for i in candidates]), rest
        for i in candidates:
            extra = min(bound - holding[i], max(1, budget * portions[i] // whole), rest)
            holding[i] = holding[i] + extra
            rest = rest - extra
    return np.array([bound] + holding)


def ragged(own_key, count, total, limit, skew):
    if count == 2:
        one = jax.random.randint(own_key, (), max(1, total - limit), min(limit, total - 1) + 1)
        return jnp.stack([one, total - one])
    tallies = jnp.asarray(profile(count, total, limit, skew), jnp.int32)
    twos = (count - 1) // 2
    giver, sink = tallies[1:1 + 2 * twos:2], tallies[2:2 + 2 * twos:2]
    room = jnp.minimum(giver - 1, limit - sink)
    passed = jax.random.randint(jax.random.fold_in(own_key, 1), (twos,), 0, 1 << 20) % (room + 1)
    tallies = tallies.at[1:1 + 2 * twos:2].set(giver - passed).at[2:2 + 2 * twos:2].set(sink + passed)
    return tallies[jax.random.permutation(jax.random.fold_in(own_key, 2), count)]


def gaussian(rng, dims, spread, reach, split=(), kind=jnp.bfloat16):
    drawn = jax.random.normal(rng, dims, jnp.float32) * spread
    if len(split) > 0:
        drawn = shard_levels(rng, dims, split, -0.22, 0.18) * drawn
    return jnp.clip(drawn, min=-reach, max=reach).astype(kind)


def setup_inputs(seed: int = 0) -> dict:
    streams_of = jax.random.split(jax.random.key(seed), 13)
    tokens = gaussian(streams_of[0], (TOKENS, D), 1.0, 6.0, ((0, 32),))
    seg_ids = jnp.searchsorted(jnp.cumsum(ragged(streams_of[1], 3 * TOKENS // LENGTH, TOKENS, LENGTH, 1)), jnp.arange(TOKENS), side="right").astype(jnp.int32)
    norm_in_w = jnp.clip(1.0 + 0.1 * jax.random.normal(streams_of[2], (D,), jnp.float32), 0.5, 1.5).astype(jnp.bfloat16)
    in_proj = gaussian(streams_of[3], (D, DPROJ), D ** -0.5, 0.21875, ((0, 8),))
    conv_w = gaussian(streams_of[4], (DCONV, CONVDIM), DCONV ** -0.5, 3.0, ((1, 8),))
    conv_b = gaussian(streams_of[5], (CONVDIM,), 0.3, 1.796875, ((0, 8),))
    a_log = jnp.clip(jax.random.uniform(streams_of[6], (NH,), jnp.float32, 0.0, 2.7), 0.0, 2.7)
    skip_d = jnp.clip(jax.random.uniform(streams_of[7], (NH,), jnp.float32, 0.5, 1.5), 0.5, 1.5)
    dt_bias = jnp.clip(jax.random.uniform(streams_of[8], (NH,), jnp.float32, -6.5, -2.5), -6.5, -2.5)
    gnorm_w = jnp.clip(1.0 + 0.1 * jax.random.normal(streams_of[9], (DIN,), jnp.float32), 0.5, 1.5).astype(jnp.bfloat16)
    out_proj = gaussian(streams_of[10], (DIN, D), DIN ** -0.5, 0.15625, ((0, 8),))
    cotangent = gaussian(streams_of[11], (TOKENS, D), 1.0, 6.0, ((0, 32),))
    return {"tokens": tokens, "seg_ids": seg_ids, "norm_in_w": norm_in_w, "in_proj": in_proj, "conv_w": conv_w, "conv_b": conv_b, "a_log": a_log, "skip_d": skip_d, "dt_bias": dt_bias, "gnorm_w": gnorm_w, "out_proj": out_proj, "cotangent": cotangent}


eps = 1e-05
HIGH = lax.Precision.HIGHEST

@jax.custom_vjp
def low(v):
    return lax.optimization_barrier(v.astype(jnp.bfloat16)).astype(jnp.float32)

@jax.custom_vjp
def low_back(v):
    return v

def low_keep(v):
    return (low(v), None)

def low_pass(kept, grad):
    return (grad,)

def back_keep(v):
    return (v, None)

def back_low(kept, grad):
    return (low(grad),)
low.defvjp(low_keep, low_pass)
low_back.defvjp(back_keep, back_low)

def prenorm(values, weight):
    return values * lax.rsqrt(lax.optimization_barrier(jnp.mean(values * values, axis=-1, keepdims=True)) + eps) * weight

def block_step(carry, inputs):
    states, previous = carry
    head_input, write_vec, read_vec, step_size, log_decay, segment = inputs
    block_len = segment.shape[0]
    cumulative = jnp.cumsum(log_decay, axis=0)
    position = jnp.arange(block_len)
    visible = (position[:, None] >= position[None, :]) & (segment[:, None] == segment[None, :])
    exponent = cumulative.T[:, :, None] - cumulative.T[:, None, :]
    exponent = jnp.where(visible[None, :, :], exponent, 0.0)
    decay_terms = jnp.where(visible[None, :, :], jnp.exp(exponent), 0.0)
    read_write = jnp.dot(read_vec, write_vec.T, precision=HIGH)
    weights = decay_terms * read_write[None, :, :] * step_size.T[:, None, :]
    within = jnp.einsum('hts,shd->thd', weights, head_input, precision=HIGH)
    keep_prev = (segment == previous).astype(jnp.float32)
    carried = jnp.einsum('tn,hnd->thd', read_vec, states, precision=HIGH)
    carried = carried * (jnp.exp(cumulative) * keep_prev[:, None])[:, :, None]
    last_segment = segment[block_len - 1]
    tail_weight = jnp.exp(cumulative[block_len - 1][None, :] - cumulative) * step_size
    tail_weight = tail_weight * (segment == last_segment).astype(jnp.float32)[:, None]
    fresh_state = jnp.einsum('sn,shd->hnd', write_vec, head_input * tail_weight[:, :, None], precision=HIGH)
    still = (last_segment == previous).astype(jnp.float32)
    states = states * (jnp.exp(cumulative[block_len - 1]) * still)[:, None, None] + fresh_state
    return ((states, last_segment), within + carried)

def mixer_layer(projected, conv_weight, conv_bias, decay_log, skip_gain, step_bias, norm_gain, segment):
    length = projected.shape[0]
    gate_part = projected[:, :DIN]
    conv_in = projected[:, DIN:DIN + CONVDIM]
    step_raw = projected[:, DIN + CONVDIM:]
    conv_sum = conv_bias[None, :] + conv_weight[DCONV - 1][None, :] * conv_in
    for offset in range(1, DCONV):
        shifted = jnp.pad(conv_in, ((offset, 0), (0, 0)))[:length]
        shifted_segment = jnp.pad(segment, (offset, 0), constant_values=-1)[:length]
        same_segment = (shifted_segment == segment).astype(jnp.float32)
        conv_sum = conv_sum + conv_weight[DCONV - 1 - offset][None, :] * shifted * same_segment[:, None]
    conv_act = jax.nn.silu(conv_sum)
    head_input = conv_act[:, :DIN].reshape(length, NH, HD)
    write_vec = conv_act[:, DIN:DIN + NS]
    read_vec = conv_act[:, DIN + NS:]
    step_size = jax.nn.softplus(step_raw + step_bias[None, :])
    log_decay = -step_size * jnp.exp(decay_log)[None, :]
    blocks = length // BLOCK

    def to_blocks(values):
        return values.reshape((blocks, BLOCK) + values.shape[1:])
    initial = (jnp.zeros((NH, NS, HD), jnp.float32), jnp.array(-1, jnp.int32))
    _, outputs = lax.scan(jax.checkpoint(block_step), initial, (to_blocks(head_input), to_blocks(write_vec), to_blocks(read_vec), to_blocks(step_size), to_blocks(log_decay), to_blocks(segment)))
    mixed_heads = outputs.reshape(length, NH, HD) + skip_gain[None, :, None] * head_input
    gated = mixed_heads.reshape(length, DIN) * jax.nn.silu(gate_part)
    return gated * lax.rsqrt(lax.optimization_barrier(jnp.mean(gated * gated, axis=-1, keepdims=True)) + eps) * norm_gain

def forward_pass(values, segment, norm_in_w, in_proj, conv_w, conv_b, a_log, skip_d, dt_bias, gnorm_w, out_proj):
    normed = low(prenorm(values, norm_in_w))
    projected = low_back(jnp.dot(normed, in_proj, precision=HIGH))
    seq_count = values.shape[0] // LENGTH
    mapped = jax.vmap(mixer_layer, in_axes=(0, None, None, None, None, None, None, 0))(projected.reshape(seq_count, LENGTH, DPROJ), conv_w, conv_b, a_log, skip_d, dt_bias, gnorm_w, segment.reshape(seq_count, LENGTH))
    mixed = low(mapped.reshape(values.shape[0], DIN))
    return values + jnp.dot(mixed, out_proj, precision=HIGH)

def reference(tokens, seg_ids, norm_in_w, in_proj, conv_w, conv_b, a_log, skip_d, dt_bias, gnorm_w, out_proj, cotangent):
    params = tuple((weight.astype(jnp.float32) for weight in (norm_in_w, in_proj, conv_w, conv_b, a_log, skip_d, dt_bias, gnorm_w, out_proj)))
    group_rows = math.gcd(SEQS, 4) * LENGTH
    group_count = TOKENS // group_rows

    def group_step(totals, inputs):
        values, segment, upstream = inputs

        def forward_group(activation, *weights):
            return forward_pass(activation, segment, *weights)
        result, pullback = jax.vjp(forward_group, values.astype(jnp.float32), *params)
        grads = pullback(upstream.astype(jnp.float32))
        totals = tuple((first + second for first, second in zip(totals, grads[1:])))
        return (totals, (result.astype(jnp.bfloat16), grads[0]))
    initial = tuple((jnp.zeros_like(weight) for weight in params))
    totals, (results, grad_rows) = lax.scan(group_step, initial, (tokens.reshape(group_count, group_rows, D), seg_ids.reshape(group_count, group_rows), cotangent.reshape(group_count, group_rows, D)))
    return (results.reshape(TOKENS, D), grad_rows.reshape(TOKENS, D), totals[0], totals[1], totals[2], totals[3], totals[4], totals[5], totals[6], totals[7], totals[8])
```

```python
import jax
import jax.numpy as jnp
from jax import lax
from jax.experimental import pallas as pl
from jax.experimental.pallas import tpu as pltpu
from jax.sharding import PartitionSpec as P

DIN = 1536
NH = 24
HD = 64
NS = 128
DCONV = 4
BLOCK = 256
CONVDIM = 1792
GROUP = 4
GROUPS = NH // GROUP
ROWS = GROUP * HD


eps = 1e-05
HIGH = lax.Precision.HIGHEST
F32 = jnp.float32
LOW = jnp.bfloat16
NN = (((1,), (0,)), ((), ()))
NT = (((1,), (1,)), ((), ()))
TN = (((0,), (0,)), ((), ()))


def prenorm(values, weight):
    return values * lax.rsqrt(jnp.mean(values * values, axis=-1, keepdims=True) + eps) * weight


def mul1(left, right, dims):
    return lax.dot_general(
        left.astype(LOW), right.astype(LOW), dims, preferred_element_type=F32
    )


def halves(values):
    top = values.astype(LOW)
    return top, (values - top.astype(F32)).astype(LOW)


def mul3(left, right, dims):
    left_top, left_rest = halves(left)
    right_top, right_rest = halves(right)
    return (
        mul1(left_top, right_top, dims)
        + mul1(left_top, right_rest, dims)
        + mul1(left_rest, right_top, dims)
    )


def block_setup(write_ref, read_ref, segrow_ref, segcol_ref, product, bias):
    product[...] = mul3(write_ref[...], read_ref[...], TN)
    source = lax.broadcasted_iota(jnp.int32, (BLOCK, BLOCK), 0)
    target = lax.broadcasted_iota(jnp.int32, (BLOCK, BLOCK), 1)
    visible = (target >= source) & (segcol_ref[...] == segrow_ref[...])
    bias[...] = jnp.where(visible, 0.0, -1e30)


def stack_rows(pieces):
    return jnp.concatenate(pieces, axis=0)


def scan_forward(
    head_ref, write_ref, read_ref, step_ref, cum_ref, cumcol_ref, keep_ref, tail_ref,
    segrow_ref, segcol_ref, out_ref, before_ref, states, product, bias
):
    block, group = pl.program_id(0), pl.program_id(1)

    @pl.when(group == 0)
    def _():
        block_setup(write_ref, read_ref, segrow_ref, segcol_ref, product, bias)

    @pl.when(block == 0)
    def _():
        states[group] = jnp.zeros((ROWS, NS), F32)

    before = states[group]
    before_ref[0] = before
    carried = mul3(before, read_ref[...], NN)
    weighted, decays = [], []
    for j in range(GROUP):
        rows = slice(j * HD, (j + 1) * HD)
        cum = cum_ref[j]
        decay = jnp.exp(cum) * keep_ref[...]
        terms = jnp.exp(cum - cumcol_ref[0][:, j : j + 1] + bias[...])
        stepped = head_ref[rows, :] * step_ref[j]
        out_ref[rows, :] = mul1(stepped, terms * product[...], NN) + carried[rows, :] * decay
        weighted.append(stepped * (jnp.exp(cum[:, BLOCK - 1 :] - cum) * tail_ref[...]))
        decays.append(jnp.broadcast_to(decay[:, BLOCK - 1 :], (HD, 1)))
    states[group] = before * stack_rows(decays) + mul3(stack_rows(weighted), write_ref[...], NT)


def scan_backward(
    head_ref, write_ref, read_ref, step_ref, cum_ref, cumcol_ref, keep_ref, tail_ref,
    segrow_ref, segcol_ref, before_ref, grad_ref, ghead_ref, gwrite_ref, gread_ref,
    gstep_ref, gcum_ref, gcumcol_ref, gstates, product, bias, gproduct
):
    block, group = pl.program_id(0), pl.program_id(1)

    @pl.when(group == 0)
    def _():
        block_setup(write_ref, read_ref, segrow_ref, segcol_ref, product, bias)
        gproduct[...] = jnp.zeros((BLOCK, BLOCK), F32)
        gwrite_ref[...] = jnp.zeros((NS, BLOCK), F32)
        gread_ref[...] = jnp.zeros((NS, BLOCK), F32)

    @pl.when(block == 0)
    def _():
        gstates[group] = jnp.zeros((ROWS, NS), F32)

    before = before_ref[0]
    after = gstates[group]
    write, read = write_ref[...], read_ref[...]
    carried = mul3(before, read, NN)
    gfresh = mul3(after, write, NN)
    state_terms = before * after
    lane = lax.broadcasted_iota(jnp.int32, (1, BLOCK), 1)
    gcarried, weighted, decays = [], [], []
    for j in range(GROUP):
        rows = slice(j * HD, (j + 1) * HD)
        cum, step = cum_ref[j], step_ref[j]
        head, grad = head_ref[rows, :], grad_ref[rows, :]
        decay = jnp.exp(cum) * keep_ref[...]
        tail = jnp.exp(cum[:, BLOCK - 1 :] - cum) * tail_ref[...]
        terms = jnp.exp(cum - cumcol_ref[0][:, j : j + 1] + bias[...])
        stepped = head * step
        weights = terms * product[...]
        head_top, head_rest = halves(stepped)
        grad_top, grad_rest = halves(grad)
        gweights = mul1(
            stack_rows([head_top, head_top, head_rest]),
            stack_rows([grad_top, grad_rest, grad_top]),
            TN,
        )
        gproduct[...] += gweights * terms
        paired = gweights * weights
        fresh = gfresh[rows, :] * tail
        gstepped = mul1(grad_top, weights, NT) + fresh
        ghead_ref[rows, :] = gstepped * step
        gstep_ref[j] = jnp.sum(gstepped * head, axis=0, keepdims=True)
        fresh_terms = jnp.sum(fresh * stepped, axis=0, keepdims=True)
        last = jnp.sum(fresh_terms, axis=1, keepdims=True) + decay[:, BLOCK - 1 :] * jnp.sum(
            jnp.sum(state_terms[rows, :], axis=0, keepdims=True), axis=1, keepdims=True
        )
        gcum_ref[j] = (
            jnp.sum(paired, axis=0, keepdims=True)
            + jnp.sum(grad * carried[rows, :], axis=0, keepdims=True) * decay
            - fresh_terms
            + jnp.where(lane == BLOCK - 1, last, 0.0)
        )
        gcumcol_ref[0, :, j : j + 1] = jnp.sum(paired, axis=1, keepdims=True)
        gcarried.append(grad * decay)
        weighted.append(stepped * tail)
        decays.append(jnp.broadcast_to(decay[:, BLOCK - 1 :], (HD, 1)))
    gcarried = stack_rows(gcarried)
    gstates[group] = after * stack_rows(decays) + mul3(gcarried, read, NT)
    gread_ref[...] += mul3(before, gcarried, TN)
    gwrite_ref[...] += mul3(after, stack_rows(weighted), TN)

    @pl.when(group == GROUPS - 1)
    def _():
        gread_ref[...] += mul3(write, gproduct[...], NN)
        gwrite_ref[...] += mul3(read, gproduct[...], NT)


def scan_specs(at):
    row = pl.BlockSpec((GROUP, 1, BLOCK), lambda i, g: (g, 0, at(i)))
    line = pl.BlockSpec((1, BLOCK), lambda i, g: (0, at(i)))
    column = pl.BlockSpec((1, BLOCK, GROUP), lambda i, g: (g, at(i), 0))
    heads = pl.BlockSpec((ROWS, BLOCK), lambda i, g: (g, at(i)))
    write = pl.BlockSpec((NS, BLOCK), lambda i, g: (DIN // NS, at(i)))
    read = pl.BlockSpec((NS, BLOCK), lambda i, g: (DIN // NS + 1, at(i)))
    segcol = pl.BlockSpec((BLOCK, 1), lambda i, g: (at(i), 0))
    before = pl.BlockSpec((1, ROWS, NS), lambda i, g: (at(i), g, 0))
    vector = pl.BlockSpec((NS, BLOCK), lambda i, g: (0, at(i)))
    shared = [heads, write, read, row, row, column, line, line, line, segcol]
    return shared, row, column, heads, before, vector


PARAMS = dict(vmem_limit_bytes=32 * 1024 * 1024)


def run_forward(operands, length):
    blocks = length // BLOCK
    shared, row, column, heads, before, vector = scan_specs(lambda i: i)
    square = pltpu.VMEM((BLOCK, BLOCK), F32)
    return pl.pallas_call(
        scan_forward,
        grid=(blocks, GROUPS),
        in_specs=shared,
        out_specs=[heads, before],
        out_shape=[
            jax.ShapeDtypeStruct((DIN, length), F32),
            jax.ShapeDtypeStruct((blocks, DIN, NS), F32),
        ],
        scratch_shapes=[pltpu.VMEM((GROUPS, ROWS, NS), F32), square, square],
        compiler_params=pltpu.CompilerParams(**PARAMS),
        cost_estimate=pl.CostEstimate(
            flops=3 * 10**9, bytes_accessed=20 * 10**6, transcendentals=7 * 10**6
        ),
    )(*operands)


def run_backward(operands, before_states, grad, length):
    blocks = length // BLOCK
    shared, row, column, heads, before, vector = scan_specs(lambda i: blocks - 1 - i)
    square = pltpu.VMEM((BLOCK, BLOCK), F32)
    return pl.pallas_call(
        scan_backward,
        grid=(blocks, GROUPS),
        in_specs=shared + [before, heads],
        out_specs=[heads, vector, vector, row, row, column],
        out_shape=[
            jax.ShapeDtypeStruct((DIN, length), F32),
            jax.ShapeDtypeStruct((NS, length), F32),
            jax.ShapeDtypeStruct((NS, length), F32),
            jax.ShapeDtypeStruct((NH, 1, length), F32),
            jax.ShapeDtypeStruct((NH, 1, length), F32),
            jax.ShapeDtypeStruct((GROUPS, length, GROUP), F32),
        ],
        scratch_shapes=[pltpu.VMEM((GROUPS, ROWS, NS), F32), square, square, square],
        compiler_params=pltpu.CompilerParams(**PARAMS),
        cost_estimate=pl.CostEstimate(
            flops=40 * 10**9, bytes_accessed=30 * 10**6, transcendentals=7 * 10**6
        ),
    )(*operands, before_states, grad)


def conv_and_steps(conv_in, step_raw, conv_weight, conv_bias, decay_log, step_bias, segment):
    length = conv_in.shape[1]
    conv_sum = conv_bias[:, None] + conv_weight[DCONV - 1][:, None] * conv_in
    for offset in range(1, DCONV):
        shifted = jnp.pad(conv_in, ((0, 0), (offset, 0)))[:, :length]
        shifted_segment = jnp.pad(segment, (offset, 0), constant_values=-1)[:length]
        same_segment = (shifted_segment == segment).astype(F32)
        conv_sum = (
            conv_sum + conv_weight[DCONV - 1 - offset][:, None] * shifted * same_segment[None, :]
        )
    conv_act = jax.nn.silu(conv_sum)
    step_size = jax.nn.softplus(step_raw + step_bias[:, None])
    log_decay = -step_size * jnp.exp(decay_log)[:, None]
    upto = jnp.triu(jnp.ones((BLOCK, BLOCK), F32))
    cumulative = jnp.dot(log_decay.reshape(-1, BLOCK), upto, precision=HIGH)
    return conv_act, step_size, cumulative.reshape(NH, length)


def gate_and_norm(scanned, head_input, gate_part, skip_gain, norm_gain):
    length = scanned.shape[1]
    skipped = skip_gain[:, None, None] * head_input.reshape(NH, HD, length)
    mixed_heads = scanned + skipped.reshape(DIN, length)
    gated = mixed_heads * jax.nn.silu(gate_part)
    return (
        gated * lax.rsqrt(jnp.mean(gated * gated, axis=0, keepdims=True) + eps) * norm_gain[:, None]
    )


def contract_rows(left, right):
    return lax.dot_general(
        left, right, (((0,), (0,)), ((), ())), preferred_element_type=jnp.float32
    )


def contract_cols(left, right):
    return lax.dot_general(
        left, right, (((1,), (1,)), ((), ())), preferred_element_type=jnp.float32
    )


def contract_cross(left, right):
    return lax.dot_general(
        left, right, (((0,), (1,)), ((), ())), preferred_element_type=jnp.float32
    )


def to_owner(grad):
    return lax.psum_scatter(grad.astype(LOW), "shard", scatter_dimension=0, tiled=True)


def on_device(
    tokens,
    seg_ids,
    norm_in_w,
    in_proj,
    conv_w,
    conv_b,
    a_log,
    skip_d,
    dt_bias,
    gnorm_w,
    out_proj,
    cotangent,
):
    length = tokens.shape[0]
    me = lax.axis_index("shard")
    n_in, n_conv, n_gnorm = norm_in_w.shape[0], conv_b.shape[0], gnorm_w.shape[0]
    small = jnp.concatenate([norm_in_w, conv_w.reshape(-1), conv_b, gnorm_w])
    small_full = lax.all_gather(small, "shard", axis=0, tiled=False)
    inproj_full = lax.all_gather(in_proj, "shard", axis=0, tiled=True)
    outproj_full = lax.all_gather(out_proj, "shard", axis=0, tiled=True)
    small_full = small_full.astype(F32)
    shards = small_full.shape[0]
    norm_full = small_full[:, :n_in].reshape(-1)
    conv_full = small_full[:, n_in : n_in + DCONV * n_conv]
    conv_full = conv_full.reshape(shards, DCONV, n_conv).transpose(1, 0, 2).reshape(DCONV, -1)
    start = n_in + DCONV * n_conv
    convb_full = small_full[:, start : start + n_conv].reshape(-1)
    gnorm_full = small_full[:, start + n_conv :].reshape(-1)

    activation = tokens.astype(F32)
    normed, norm_back = jax.vjp(prenorm, activation, norm_full)
    normed_low = normed.astype(LOW)
    projected = contract_cross(inproj_full, normed_low)
    gate_part = projected[:DIN]

    segrow = seg_ids.reshape(-1, BLOCK)
    lasts = segrow[:, BLOCK - 1 :]
    previous = jnp.concatenate([jnp.full((1, 1), -1, lasts.dtype), lasts[:-1]], axis=0)
    keep = (segrow == previous).astype(F32).reshape(1, length)
    tail = (segrow == lasts).astype(F32).reshape(1, length)

    (conv_act, step_size, cumulative), conv_back = jax.vjp(
        lambda *args: conv_and_steps(*args, seg_ids),
        projected[DIN : DIN + CONVDIM],
        projected[DIN + CONVDIM :],
        conv_full,
        convb_full,
        a_log,
        dt_bias,
    )
    cumcol = cumulative.reshape(GROUPS, GROUP, length).transpose(0, 2, 1)
    operands = (
        conv_act,
        conv_act,
        conv_act,
        step_size.reshape(NH, 1, length),
        cumulative.reshape(NH, 1, length),
        cumcol,
        keep,
        tail,
        seg_ids.reshape(1, length),
        seg_ids.reshape(length, 1),
    )
    scanned, before_states = run_forward(operands, length)
    mixed_out, gate_back = jax.vjp(
        gate_and_norm, scanned, conv_act[:DIN], gate_part, skip_d, gnorm_full
    )
    mixed_low = mixed_out.astype(LOW)
    output = (activation + contract_rows(mixed_low, outproj_full)).astype(LOW)
    grad_out = jnp.dot(mixed_low, cotangent, preferred_element_type=F32)
    share_out = to_owner(grad_out)
    grad_mixed = contract_cols(outproj_full, cotangent)
    gscanned, ghead_skip, ggate, grad_skip, grad_gnorm = gate_back(grad_mixed)
    ggate_low = ggate.astype(LOW)
    share_gate = to_owner(contract_cross(normed_low, ggate_low))
    grad_normed = contract_cross(ggate_low, inproj_full[:, :DIN])

    ghead, gwrite, gread, gstep, gcum, gcumcol = run_backward(
        operands, before_states, gscanned, length
    )
    gcumulative = gcum.reshape(NH, length) - gcumcol.transpose(0, 2, 1).reshape(NH, length)
    gconv_act = jnp.concatenate([ghead + ghead_skip, gwrite, gread], axis=0)
    gconv_in, gstep_raw, grad_conv, grad_convb, grad_alog, grad_step = conv_back(
        (gconv_act, gstep.reshape(NH, length), gcumulative)
    )
    grest_low = jnp.concatenate([gconv_in.astype(LOW), gstep_raw.astype(LOW)], axis=0)
    share_rest = to_owner(contract_cross(normed_low, grest_low))
    grad_normed = grad_normed + contract_cross(grest_low, inproj_full[:, DIN:])
    grad_activation, grad_norm = norm_back(grad_normed)
    grad_tokens = cotangent.astype(F32) + grad_activation

    parts = [grad_norm, grad_conv.reshape(-1), grad_convb, grad_gnorm, grad_alog, grad_skip, grad_step]
    sums = lax.psum(jnp.concatenate(parts), ("rep", "shard"))
    taken, place = [], 0
    for part in parts:
        taken.append(sums[place : place + part.shape[0]])
        place += part.shape[0]
    own = lambda full, count: lax.dynamic_slice_in_dim(full, me * count, count, axis=-1)
    total_out = lax.psum(share_out, "rep").astype(F32)
    total_gate, total_rest = lax.psum((share_gate, share_rest), "rep")
    total_in = jnp.concatenate([total_gate.astype(F32), total_rest.astype(F32)], axis=1)
    return (
        output,
        grad_tokens,
        own(taken[0], n_in),
        total_in,
        own(taken[1].reshape(DCONV, -1), n_conv),
        own(taken[2], n_conv),
        taken[4],
        taken[5],
        taken[6],
        own(taken[3], n_gnorm),
        total_out,
    )


def solution(mesh):
    placed = (
        P(("rep", "shard"), None),
        P(("rep", "shard")),
        P("shard"),
        P("shard", None),
        P(None, "shard"),
        P("shard"),
        P(),
        P(),
        P(),
        P("shard"),
        P("shard", None),
        P(("rep", "shard"), None),
    )
    return jax.shard_map(
        on_device,
        mesh=mesh,
        in_specs=placed,
        out_specs=(
            P(("rep", "shard"), None),
            P(("rep", "shard"), None),
            P("shard"),
            P("shard", None),
            P(None, "shard"),
            P("shard"),
            P(),
            P(),
            P(),
            P("shard"),
            P("shard", None),
        ),
        check_vma=False,
    )
```

```python
import jax
import jax.numpy as jnp
from jax import lax
from jax.experimental import pallas as pl
from jax.experimental.pallas import tpu as pltpu
from jax.sharding import PartitionSpec as P

DIN = 1536
NH = 24
HD = 64
NS = 128
DCONV = 4
BLOCK = 256
CONVDIM = 1792
GROUP = 4
GROUPS = NH // GROUP
ROWS = GROUP * HD


eps = 1e-05
HIGH = lax.Precision.HIGHEST
F32 = jnp.float32
LOW = jnp.bfloat16
NN = (((1,), (0,)), ((), ()))
NT = (((1,), (1,)), ((), ()))
TN = (((0,), (0,)), ((), ()))


def prenorm(values, weight):
    return values * lax.rsqrt(jnp.mean(values * values, axis=-1, keepdims=True) + eps) * weight


def mul1(left, right, dims):
    return lax.dot_general(
        left.astype(LOW), right.astype(LOW), dims, preferred_element_type=F32
    )


def halves(values):
    top = values.astype(LOW)
    return top, (values - top.astype(F32)).astype(LOW)


def mul3(left, right, dims):
    left_top, left_rest = halves(left)
    right_top, right_rest = halves(right)
    return (
        mul1(left_top, right_top, dims)
        + mul1(left_top, right_rest, dims)
        + mul1(left_rest, right_top, dims)
    )


def block_setup(write_ref, read_ref, segrow_ref, segcol_ref, product, bias):
    product[...] = mul3(write_ref[...], read_ref[...], TN)
    source = lax.broadcasted_iota(jnp.int32, (BLOCK, BLOCK), 0)
    target = lax.broadcasted_iota(jnp.int32, (BLOCK, BLOCK), 1)
    visible = (target >= source) & (segcol_ref[...] == segrow_ref[...])
    bias[...] = jnp.where(visible, 0.0, -1e30)


def stack_rows(pieces):
    return jnp.concatenate(pieces, axis=0)


def scan_forward(
    head_ref, write_ref, read_ref, step_ref, cum_ref, cumcol_ref, keep_ref, tail_ref,
    segrow_ref, segcol_ref, out_ref, before_ref, states, product, bias
):
    block, group = pl.program_id(0), pl.program_id(1)

    @pl.when(group == 0)
    def _():
        block_setup(write_ref, read_ref, segrow_ref, segcol_ref, product, bias)

    @pl.when(block == 0)
    def _():
        states[group] = jnp.zeros((ROWS, NS), F32)

    before = states[group]
    before_ref[0] = before
    carried = mul3(before, read_ref[...], NN)
    weighted, decays = [], []
    for j in range(GROUP):
        rows = slice(j * HD, (j + 1) * HD)
        cum = cum_ref[j]
        decay = jnp.exp(cum) * keep_ref[...]
        terms = jnp.exp(cum - cumcol_ref[0][:, j : j + 1] + bias[...])
        stepped = head_ref[rows, :] * step_ref[j]
        out_ref[rows, :] = mul1(stepped, terms * product[...], NN) + carried[rows, :] * decay
        weighted.append(stepped * (jnp.exp(cum[:, BLOCK - 1 :] - cum) * tail_ref[...]))
        decays.append(jnp.broadcast_to(decay[:, BLOCK - 1 :], (HD, 1)))
    states[group] = before * stack_rows(decays) + mul3(stack_rows(weighted), write_ref[...], NT)


def scan_backward(
    head_ref, write_ref, read_ref, step_ref, cum_ref, cumcol_ref, keep_ref, tail_ref,
    segrow_ref, segcol_ref, before_ref, grad_ref, ghead_ref, gwrite_ref, gread_ref,
    gstep_ref, gcum_ref, gcumcol_ref, gstates, product, bias, gproduct
):
    block, group = pl.program_id(0), pl.program_id(1)

    @pl.when(group == 0)
    def _():
        block_setup(write_ref, read_ref, segrow_ref, segcol_ref, product, bias)
        gproduct[...] = jnp.zeros((BLOCK, BLOCK), F32)
        gwrite_ref[...] = jnp.zeros((NS, BLOCK), F32)
        gread_ref[...] = jnp.zeros((NS, BLOCK), F32)

    @pl.when(block == 0)
    def _():
        gstates[group] = jnp.zeros((ROWS, NS), F32)

    before = before_ref[0]
    after = gstates[group]
    write, read = write_ref[...], read_ref[...]
    carried = mul3(before, read, NN)
    gfresh = mul3(after, write, NN)
    state_terms = before * after
    lane = lax.broadcasted_iota(jnp.int32, (1, BLOCK), 1)
    gcarried, weighted, decays = [], [], []
    for j in range(GROUP):
        rows = slice(j * HD, (j + 1) * HD)
        cum, step = cum_ref[j], step_ref[j]
        head, grad = head_ref[rows, :], grad_ref[rows, :]
        decay = jnp.exp(cum) * keep_ref[...]
        tail = jnp.exp(cum[:, BLOCK - 1 :] - cum) * tail_ref[...]
        terms = jnp.exp(cum - cumcol_ref[0][:, j : j + 1] + bias[...])
        stepped = head * step
        weights = terms * product[...]
        head_top, head_rest = halves(stepped)
        grad_top, grad_rest = halves(grad)
        gweights = mul1(
            stack_rows([head_top, head_top, head_rest]),
            stack_rows([grad_top, grad_rest, grad_top]),
            TN,
        )
        gproduct[...] += gweights * terms
        paired = gweights * weights
        fresh = gfresh[rows, :] * tail
        gstepped = mul1(grad_top, weights, NT) + fresh
        ghead_ref[rows, :] = gstepped * step
        gstep_ref[j] = jnp.sum(gstepped * head, axis=0, keepdims=True)
        fresh_terms = jnp.sum(fresh * stepped, axis=0, keepdims=True)
        last = jnp.sum(fresh_terms, axis=1, keepdims=True) + decay[:, BLOCK - 1 :] * jnp.sum(
            jnp.sum(state_terms[rows, :], axis=0, keepdims=True), axis=1, keepdims=True
        )
        gcum_ref[j] = (
            jnp.sum(paired, axis=0, keepdims=True)
            + jnp.sum(grad * carried[rows, :], axis=0, keepdims=True) * decay
            - fresh_terms
            + jnp.where(lane == BLOCK - 1, last, 0.0)
        )
        gcumcol_ref[0, :, j : j + 1] = jnp.sum(paired, axis=1, keepdims=True)
        gcarried.append(grad * decay)
        weighted.append(stepped * tail)
        decays.append(jnp.broadcast_to(decay[:, BLOCK - 1 :], (HD, 1)))
    gcarried = stack_rows(gcarried)
    gstates[group] = after * stack_rows(decays) + mul3(gcarried, read, NT)
    gread_ref[...] += mul3(before, gcarried, TN)
    gwrite_ref[...] += mul3(after, stack_rows(weighted), TN)

    @pl.when(group == GROUPS - 1)
    def _():
        gread_ref[...] += mul3(write, gproduct[...], NN)
        gwrite_ref[...] += mul3(read, gproduct[...], NT)


def scan_specs(at):
    row = pl.BlockSpec((GROUP, 1, BLOCK), lambda i, g: (g, 0, at(i)))
    line = pl.BlockSpec((1, BLOCK), lambda i, g: (0, at(i)))
    column = pl.BlockSpec((1, BLOCK, GROUP), lambda i, g: (g, at(i), 0))
    heads = pl.BlockSpec((ROWS, BLOCK), lambda i, g: (g, at(i)))
    write = pl.BlockSpec((NS, BLOCK), lambda i, g: (DIN // NS, at(i)))
    read = pl.BlockSpec((NS, BLOCK), lambda i, g: (DIN // NS + 1, at(i)))
    segcol = pl.BlockSpec((BLOCK, 1), lambda i, g: (at(i), 0))
    before = pl.BlockSpec((1, ROWS, NS), lambda i, g: (at(i), g, 0))
    vector = pl.BlockSpec((NS, BLOCK), lambda i, g: (0, at(i)))
    shared = [heads, write, read, row, row, column, line, line, line, segcol]
    return shared, row, column, heads, before, vector


PARAMS = dict(vmem_limit_bytes=32 * 1024 * 1024)


def run_forward(operands, length):
    blocks = length // BLOCK
    shared, row, column, heads, before, vector = scan_specs(lambda i: i)
    square = pltpu.VMEM((BLOCK, BLOCK), F32)
    return pl.pallas_call(
        scan_forward,
        grid=(blocks, GROUPS),
        in_specs=shared,
        out_specs=[heads, before],
        out_shape=[
            jax.ShapeDtypeStruct((DIN, length), F32),
            jax.ShapeDtypeStruct((blocks, DIN, NS), F32),
        ],
        scratch_shapes=[pltpu.VMEM((GROUPS, ROWS, NS), F32), square, square],
        compiler_params=pltpu.CompilerParams(**PARAMS),
        cost_estimate=pl.CostEstimate(
            flops=3 * 10**9, bytes_accessed=20 * 10**6, transcendentals=7 * 10**6
        ),
    )(*operands)


def run_backward(operands, before_states, grad, length):
    blocks = length // BLOCK
    shared, row, column, heads, before, vector = scan_specs(lambda i: blocks - 1 - i)
    square = pltpu.VMEM((BLOCK, BLOCK), F32)
    return pl.pallas_call(
        scan_backward,
        grid=(blocks, GROUPS),
        in_specs=shared + [before, heads],
        out_specs=[heads, vector, vector, row, row, column],
        out_shape=[
            jax.ShapeDtypeStruct((DIN, length), F32),
            jax.ShapeDtypeStruct((NS, length), F32),
            jax.ShapeDtypeStruct((NS, length), F32),
            jax.ShapeDtypeStruct((NH, 1, length), F32),
            jax.ShapeDtypeStruct((NH, 1, length), F32),
            jax.ShapeDtypeStruct((GROUPS, length, GROUP), F32),
        ],
        scratch_shapes=[pltpu.VMEM((GROUPS, ROWS, NS), F32), square, square, square],
        compiler_params=pltpu.CompilerParams(**PARAMS),
        cost_estimate=pl.CostEstimate(
            flops=40 * 10**9, bytes_accessed=30 * 10**6, transcendentals=7 * 10**6
        ),
    )(*operands, before_states, grad)


def conv_and_steps(conv_in, step_raw, conv_weight, conv_bias, decay_log, step_bias, segment):
    length = conv_in.shape[1]
    conv_sum = conv_bias[:, None] + conv_weight[DCONV - 1][:, None] * conv_in
    for offset in range(1, DCONV):
        shifted = jnp.pad(conv_in, ((0, 0), (offset, 0)))[:, :length]
        shifted_segment = jnp.pad(segment, (offset, 0), constant_values=-1)[:length]
        same_segment = (shifted_segment == segment).astype(F32)
        conv_sum = (
            conv_sum + conv_weight[DCONV - 1 - offset][:, None] * shifted * same_segment[None, :]
        )
    conv_act = jax.nn.silu(conv_sum)
    step_size = jax.nn.softplus(step_raw + step_bias[:, None])
    log_decay = -step_size * jnp.exp(decay_log)[:, None]
    upto = jnp.triu(jnp.ones((BLOCK, BLOCK), F32))
    cumulative = jnp.dot(log_decay.reshape(-1, BLOCK), upto, precision=HIGH)
    return conv_act, step_size, cumulative.reshape(NH, length)


def gate_and_norm(scanned, head_input, gate_part, skip_gain, norm_gain):
    length = scanned.shape[1]
    skipped = skip_gain[:, None, None] * head_input.reshape(NH, HD, length)
    mixed_heads = scanned + skipped.reshape(DIN, length)
    gated = mixed_heads * jax.nn.silu(gate_part)
    return (
        gated * lax.rsqrt(jnp.mean(gated * gated, axis=0, keepdims=True) + eps) * norm_gain[:, None]
    )


def contract_rows(left, right):
    return lax.dot_general(
        left, right, (((0,), (0,)), ((), ())), preferred_element_type=jnp.float32
    )


def contract_cols(left, right):
    return lax.dot_general(
        left, right, (((1,), (1,)), ((), ())), preferred_element_type=jnp.float32
    )


def contract_cross(left, right):
    return lax.dot_general(
        left, right, (((0,), (1,)), ((), ())), preferred_element_type=jnp.float32
    )


def to_owner(grad):
    return lax.psum_scatter(grad.astype(LOW), "shard", scatter_dimension=0, tiled=True)


def partners(axis, step):
    return [(i, i ^ step) for i in range(lax.axis_size(axis))]


def steps_of(axis):
    return [1 << bit for bit in range((lax.axis_size(axis) - 1).bit_length())]


def owner_total(grad):
    me = lax.axis_index("shard")
    count = lax.axis_size("shard")
    rows, columns = grad.shape[0] // count, grad.shape[1]
    left = count
    for step in steps_of("shard"):
        left //= 2
        bit = (me // step) % 2
        pairs = grad.reshape(left, 2, rows, columns)
        mine = lax.dynamic_index_in_dim(pairs, bit, 1, keepdims=False)
        other = lax.dynamic_index_in_dim(pairs, 1 - bit, 1, keepdims=False)
        got = lax.ppermute(other.astype(LOW), "shard", partners("shard", step))
        grad = mine + got.astype(F32)
    grad = grad.reshape(rows, columns)
    for step in steps_of("rep"):
        sent = grad.astype(LOW)
        got = lax.ppermute(sent, "rep", partners("rep", step))
        grad = sent.astype(F32) + got.astype(F32)
    return grad


def sum_everywhere(values):
    for axis in ("shard", "rep"):
        for step in steps_of(axis):
            values = values + lax.ppermute(values, axis, partners(axis, step))
    return values


def on_device(
    tokens,
    seg_ids,
    norm_in_w,
    in_proj,
    conv_w,
    conv_b,
    a_log,
    skip_d,
    dt_bias,
    gnorm_w,
    out_proj,
    cotangent,
):
    length = tokens.shape[0]
    me = lax.axis_index("shard")
    n_in, n_conv, n_gnorm = norm_in_w.shape[0], conv_b.shape[0], gnorm_w.shape[0]
    small = jnp.concatenate([norm_in_w, conv_w.reshape(-1), conv_b, gnorm_w])
    width = in_proj.shape[1]
    extra = -(-small.shape[0] // width)
    small = jnp.pad(small, (0, extra * width - small.shape[0])).reshape(extra, width)
    joined = lax.all_gather(jnp.concatenate([in_proj, small]), "shard", axis=0, tiled=False)
    inproj_full = joined[:, :n_in].reshape(-1, width)
    small_full = joined[:, n_in:].reshape(joined.shape[0], -1)
    outproj_full = lax.all_gather(out_proj, "shard", axis=0, tiled=True)
    small_full = small_full.astype(F32)
    shards = small_full.shape[0]
    norm_full = small_full[:, :n_in].reshape(-1)
    conv_full = small_full[:, n_in : n_in + DCONV * n_conv]
    conv_full = conv_full.reshape(shards, DCONV, n_conv).transpose(1, 0, 2).reshape(DCONV, -1)
    start = n_in + DCONV * n_conv
    convb_full = small_full[:, start : start + n_conv].reshape(-1)
    start += n_conv
    gnorm_full = small_full[:, start : start + n_gnorm].reshape(-1)

    activation = tokens.astype(F32)
    normed, norm_back = jax.vjp(prenorm, activation, norm_full)
    normed_low = normed.astype(LOW)
    projected = contract_cross(inproj_full, normed_low)
    gate_part = projected[:DIN]

    segrow = seg_ids.reshape(-1, BLOCK)
    lasts = segrow[:, BLOCK - 1 :]
    previous = jnp.concatenate([jnp.full((1, 1), -1, lasts.dtype), lasts[:-1]], axis=0)
    keep = (segrow == previous).astype(F32).reshape(1, length)
    tail = (segrow == lasts).astype(F32).reshape(1, length)

    (conv_act, step_size, cumulative), conv_back = jax.vjp(
        lambda *args: conv_and_steps(*args, seg_ids),
        projected[DIN : DIN + CONVDIM],
        projected[DIN + CONVDIM :],
        conv_full,
        convb_full,
        a_log,
        dt_bias,
    )
    cumcol = cumulative.reshape(GROUPS, GROUP, length).transpose(0, 2, 1)
    operands = (
        conv_act,
        conv_act,
        conv_act,
        step_size.reshape(NH, 1, length),
        cumulative.reshape(NH, 1, length),
        cumcol,
        keep,
        tail,
        seg_ids.reshape(1, length),
        seg_ids.reshape(length, 1),
    )
    scanned, before_states = run_forward(operands, length)
    mixed_out, gate_back = jax.vjp(
        gate_and_norm, scanned, conv_act[:DIN], gate_part, skip_d, gnorm_full
    )
    mixed_low = mixed_out.astype(LOW)
    output = (activation + contract_rows(mixed_low, outproj_full)).astype(LOW)
    grad_out = jnp.dot(mixed_low, cotangent, preferred_element_type=F32)
    share_out = to_owner(grad_out)
    grad_mixed = contract_cols(outproj_full, cotangent)
    gscanned, ghead_skip, ggate, grad_skip, grad_gnorm = gate_back(grad_mixed)
    ggate_low = ggate.astype(LOW)
    share_gate = to_owner(contract_cross(normed_low, ggate_low))
    grad_normed = contract_cross(ggate_low, inproj_full[:, :DIN])

    ghead, gwrite, gread, gstep, gcum, gcumcol = run_backward(
        operands, before_states, gscanned, length
    )
    gcumulative = gcum.reshape(NH, length) - gcumcol.transpose(0, 2, 1).reshape(NH, length)
    gconv_act = jnp.concatenate([ghead + ghead_skip, gwrite, gread], axis=0)
    gconv_in, gstep_raw, grad_conv, grad_convb, grad_alog, grad_step = conv_back(
        (gconv_act, gstep.reshape(NH, length), gcumulative)
    )
    grest_low = jnp.concatenate([gconv_in.astype(LOW), gstep_raw.astype(LOW)], axis=0)
    total_rest = owner_total(contract_cross(normed_low, grest_low))
    grad_normed = grad_normed + contract_cross(grest_low, inproj_full[:, DIN:])
    grad_activation, grad_norm = norm_back(grad_normed)
    grad_tokens = cotangent.astype(F32) + grad_activation

    parts = [grad_norm, grad_conv.reshape(-1), grad_convb, grad_gnorm, grad_alog, grad_skip, grad_step]
    sums = sum_everywhere(jnp.concatenate(parts))
    taken, place = [], 0
    for part in parts:
        taken.append(sums[place : place + part.shape[0]])
        place += part.shape[0]
    own = lambda full, count: lax.dynamic_slice_in_dim(full, me * count, count, axis=-1)
    total_out, total_gate = lax.psum((share_out, share_gate), "rep")
    total_out = total_out.astype(F32)
    total_in = jnp.concatenate([total_gate.astype(F32), total_rest], axis=1)
    return (
        output,
        grad_tokens,
        own(taken[0], n_in),
        total_in,
        own(taken[1].reshape(DCONV, -1), n_conv),
        own(taken[2], n_conv),
        taken[4],
        taken[5],
        taken[6],
        own(taken[3], n_gnorm),
        total_out,
    )


def solution(mesh):
    placed = (
        P(("rep", "shard"), None),
        P(("rep", "shard")),
        P("shard"),
        P("shard", None),
        P(None, "shard"),
        P("shard"),
        P(),
        P(),
        P(),
        P("shard"),
        P("shard", None),
        P(("rep", "shard"), None),
    )
    return jax.shard_map(
        on_device,
        mesh=mesh,
        in_specs=placed,
        out_specs=(
            P(("rep", "shard"), None),
            P(("rep", "shard"), None),
            P("shard"),
            P("shard", None),
            P(None, "shard"),
            P("shard"),
            P(),
            P(),
            P(),
            P("shard"),
            P("shard", None),
        ),
        check_vma=False,
    )
```

```python
import jax
import jax.numpy as jnp
from jax import lax
from jax.experimental import pallas as pl
from jax.experimental.pallas import tpu as pltpu
from jax.sharding import PartitionSpec as P

DIN = 1536
NH = 24
HD = 64
NS = 128
DCONV = 4
BLOCK = 256
CONVDIM = 1792
GROUP = 4
GROUPS = NH // GROUP
ROWS = GROUP * HD


eps = 1e-05
HIGH = lax.Precision.HIGHEST
F32 = jnp.float32
LOW = jnp.bfloat16
NN = (((1,), (0,)), ((), ()))
NT = (((1,), (1,)), ((), ()))
TN = (((0,), (0,)), ((), ()))


def prenorm(values, weight):
    return values * lax.rsqrt(jnp.mean(values * values, axis=-1, keepdims=True) + eps) * weight


def mul1(left, right, dims):
    return lax.dot_general(
        left.astype(LOW), right.astype(LOW), dims, preferred_element_type=F32
    )


def halves(values):
    top = values.astype(LOW)
    return top, (values - top.astype(F32)).astype(LOW)


def mul3(left, right, dims):
    left_top, left_rest = halves(left)
    right_top, right_rest = halves(right)
    return (
        mul1(left_top, right_top, dims)
        + mul1(left_top, right_rest, dims)
        + mul1(left_rest, right_top, dims)
    )


def block_setup(write_ref, read_ref, segrow_ref, segcol_ref, product, bias):
    product[...] = mul3(write_ref[...], read_ref[...], TN)
    source = lax.broadcasted_iota(jnp.int32, (BLOCK, BLOCK), 0)
    target = lax.broadcasted_iota(jnp.int32, (BLOCK, BLOCK), 1)
    visible = (target >= source) & (segcol_ref[...] == segrow_ref[...])
    bias[...] = jnp.where(visible, 0.0, -1e30)


def stack_rows(pieces):
    return jnp.concatenate(pieces, axis=0)


def scan_forward(
    head_ref, write_ref, read_ref, step_ref, cum_ref, cumcol_ref, keep_ref, tail_ref,
    segrow_ref, segcol_ref, out_ref, before_ref, states, product, bias
):
    block, group = pl.program_id(0), pl.program_id(1)

    @pl.when(group == 0)
    def _():
        block_setup(write_ref, read_ref, segrow_ref, segcol_ref, product, bias)

    @pl.when(block == 0)
    def _():
        states[group] = jnp.zeros((ROWS, NS), F32)

    before = states[group]
    before_ref[0] = before
    carried = mul3(before, read_ref[...], NN)
    weighted, decays = [], []
    for j in range(GROUP):
        rows = slice(j * HD, (j + 1) * HD)
        cum = cum_ref[j]
        decay = jnp.exp(cum) * keep_ref[...]
        terms = jnp.exp(cum - cumcol_ref[0][:, j : j + 1] + bias[...])
        stepped = head_ref[rows, :] * step_ref[j]
        out_ref[rows, :] = mul1(stepped, terms * product[...], NN) + carried[rows, :] * decay
        weighted.append(stepped * (jnp.exp(cum[:, BLOCK - 1 :] - cum) * tail_ref[...]))
        decays.append(jnp.broadcast_to(decay[:, BLOCK - 1 :], (HD, 1)))
    states[group] = before * stack_rows(decays) + mul3(stack_rows(weighted), write_ref[...], NT)


def scan_backward(
    head_ref, write_ref, read_ref, step_ref, cum_ref, cumcol_ref, keep_ref, tail_ref,
    segrow_ref, segcol_ref, before_ref, grad_ref, ghead_ref, gwrite_ref, gread_ref,
    gstep_ref, gcum_ref, gcumcol_ref, gstates, product, bias, gproduct
):
    block, group = pl.program_id(0), pl.program_id(1)

    @pl.when(group == 0)
    def _():
        block_setup(write_ref, read_ref, segrow_ref, segcol_ref, product, bias)
        gproduct[...] = jnp.zeros((BLOCK, BLOCK), F32)
        gwrite_ref[...] = jnp.zeros((NS, BLOCK), F32)
        gread_ref[...] = jnp.zeros((NS, BLOCK), F32)

    @pl.when(block == 0)
    def _():
        gstates[group] = jnp.zeros((ROWS, NS), F32)

    before = before_ref[0]
    after = gstates[group]
    write, read = write_ref[...], read_ref[...]
    carried = mul3(before, read, NN)
    gfresh = mul3(after, write, NN)
    state_terms = before * after
    lane = lax.broadcasted_iota(jnp.int32, (1, BLOCK), 1)
    gcarried, weighted, decays = [], [], []
    for j in range(GROUP):
        rows = slice(j * HD, (j + 1) * HD)
        cum, step = cum_ref[j], step_ref[j]
        head, grad = head_ref[rows, :], grad_ref[rows, :]
        decay = jnp.exp(cum) * keep_ref[...]
        tail = jnp.exp(cum[:, BLOCK - 1 :] - cum) * tail_ref[...]
        terms = jnp.exp(cum - cumcol_ref[0][:, j : j + 1] + bias[...])
        stepped = head * step
        weights = terms * product[...]
        head_top, head_rest = halves(stepped)
        grad_top, grad_rest = halves(grad)
        gweights = mul1(
            stack_rows([head_top, head_top, head_rest]),
            stack_rows([grad_top, grad_rest, grad_top]),
            TN,
        )
        gproduct[...] += gweights * terms
        paired = gweights * weights
        fresh = gfresh[rows, :] * tail
        gstepped = mul1(grad_top, weights, NT) + fresh
        ghead_ref[rows, :] = gstepped * step
        gstep_ref[j] = jnp.sum(gstepped * head, axis=0, keepdims=True)
        fresh_terms = jnp.sum(fresh * stepped, axis=0, keepdims=True)
        last = jnp.sum(fresh_terms, axis=1, keepdims=True) + decay[:, BLOCK - 1 :] * jnp.sum(
            jnp.sum(state_terms[rows, :], axis=0, keepdims=True), axis=1, keepdims=True
        )
        gcum_ref[j] = (
            jnp.sum(paired, axis=0, keepdims=True)
            + jnp.sum(grad * carried[rows, :], axis=0, keepdims=True) * decay
            - fresh_terms
            + jnp.where(lane == BLOCK - 1, last, 0.0)
        )
        gcumcol_ref[0, :, j : j + 1] = jnp.sum(paired, axis=1, keepdims=True)
        gcarried.append(grad * decay)
        weighted.append(stepped * tail)
        decays.append(jnp.broadcast_to(decay[:, BLOCK - 1 :], (HD, 1)))
    gcarried = stack_rows(gcarried)
    gstates[group] = after * stack_rows(decays) + mul3(gcarried, read, NT)
    gread_ref[...] += mul3(before, gcarried, TN)
    gwrite_ref[...] += mul3(after, stack_rows(weighted), TN)

    @pl.when(group == GROUPS - 1)
    def _():
        gread_ref[...] += mul3(write, gproduct[...], NN)
        gwrite_ref[...] += mul3(read, gproduct[...], NT)


def scan_specs(at):
    row = pl.BlockSpec((GROUP, 1, BLOCK), lambda i, g: (g, 0, at(i)))
    line = pl.BlockSpec((1, BLOCK), lambda i, g: (0, at(i)))
    column = pl.BlockSpec((1, BLOCK, GROUP), lambda i, g: (g, at(i), 0))
    heads = pl.BlockSpec((ROWS, BLOCK), lambda i, g: (g, at(i)))
    write = pl.BlockSpec((NS, BLOCK), lambda i, g: (DIN // NS, at(i)))
    read = pl.BlockSpec((NS, BLOCK), lambda i, g: (DIN // NS + 1, at(i)))
    segcol = pl.BlockSpec((BLOCK, 1), lambda i, g: (at(i), 0))
    before = pl.BlockSpec((1, ROWS, NS), lambda i, g: (at(i), g, 0))
    vector = pl.BlockSpec((NS, BLOCK), lambda i, g: (0, at(i)))
    shared = [heads, write, read, row, row, column, line, line, line, segcol]
    return shared, row, column, heads, before, vector


PARAMS = dict(vmem_limit_bytes=32 * 1024 * 1024)


def run_forward(operands, length):
    blocks = length // BLOCK
    shared, row, column, heads, before, vector = scan_specs(lambda i: i)
    square = pltpu.VMEM((BLOCK, BLOCK), F32)
    return pl.pallas_call(
        scan_forward,
        grid=(blocks, GROUPS),
        in_specs=shared,
        out_specs=[heads, before],
        out_shape=[
            jax.ShapeDtypeStruct((DIN, length), F32),
            jax.ShapeDtypeStruct((blocks, DIN, NS), F32),
        ],
        scratch_shapes=[pltpu.VMEM((GROUPS, ROWS, NS), F32), square, square],
        compiler_params=pltpu.CompilerParams(**PARAMS),
        cost_estimate=pl.CostEstimate(
            flops=3 * 10**9, bytes_accessed=20 * 10**6, transcendentals=7 * 10**6
        ),
    )(*operands)


def run_backward(operands, before_states, grad, length):
    blocks = length // BLOCK
    shared, row, column, heads, before, vector = scan_specs(lambda i: blocks - 1 - i)
    square = pltpu.VMEM((BLOCK, BLOCK), F32)
    return pl.pallas_call(
        scan_backward,
        grid=(blocks, GROUPS),
        in_specs=shared + [before, heads],
        out_specs=[heads, vector, vector, row, row, column],
        out_shape=[
            jax.ShapeDtypeStruct((DIN, length), F32),
            jax.ShapeDtypeStruct((NS, length), F32),
            jax.ShapeDtypeStruct((NS, length), F32),
            jax.ShapeDtypeStruct((NH, 1, length), F32),
            jax.ShapeDtypeStruct((NH, 1, length), F32),
            jax.ShapeDtypeStruct((GROUPS, length, GROUP), F32),
        ],
        scratch_shapes=[pltpu.VMEM((GROUPS, ROWS, NS), F32), square, square, square],
        compiler_params=pltpu.CompilerParams(**PARAMS),
        cost_estimate=pl.CostEstimate(
            flops=40 * 10**9, bytes_accessed=30 * 10**6, transcendentals=7 * 10**6
        ),
    )(*operands, before_states, grad)


def conv_and_steps(conv_in, step_raw, conv_weight, conv_bias, decay_log, step_bias, segment):
    length = conv_in.shape[1]
    conv_sum = conv_bias[:, None] + conv_weight[DCONV - 1][:, None] * conv_in
    for offset in range(1, DCONV):
        shifted = jnp.pad(conv_in, ((0, 0), (offset, 0)))[:, :length]
        shifted_segment = jnp.pad(segment, (offset, 0), constant_values=-1)[:length]
        same_segment = (shifted_segment == segment).astype(F32)
        conv_sum = (
            conv_sum + conv_weight[DCONV - 1 - offset][:, None] * shifted * same_segment[None, :]
        )
    conv_act = jax.nn.silu(conv_sum)
    step_size = jax.nn.softplus(step_raw + step_bias[:, None])
    log_decay = -step_size * jnp.exp(decay_log)[:, None]
    upto = jnp.triu(jnp.ones((BLOCK, BLOCK), F32))
    cumulative = jnp.dot(log_decay.reshape(-1, BLOCK), upto, precision=HIGH)
    return conv_act, step_size, cumulative.reshape(NH, length)


def gate_and_norm(scanned, head_input, gate_part, skip_gain, norm_gain):
    length = scanned.shape[1]
    skipped = skip_gain[:, None, None] * head_input.reshape(NH, HD, length)
    mixed_heads = scanned + skipped.reshape(DIN, length)
    gated = mixed_heads * jax.nn.silu(gate_part)
    return (
        gated * lax.rsqrt(jnp.mean(gated * gated, axis=0, keepdims=True) + eps) * norm_gain[:, None]
    )


def contract_rows(left, right):
    return lax.dot_general(
        left, right, (((0,), (0,)), ((), ())), preferred_element_type=jnp.float32
    )


def contract_cols(left, right):
    return lax.dot_general(
        left, right, (((1,), (1,)), ((), ())), preferred_element_type=jnp.float32
    )


def contract_cross(left, right):
    return lax.dot_general(
        left, right, (((0,), (1,)), ((), ())), preferred_element_type=jnp.float32
    )


def to_owner(grad):
    return lax.psum_scatter(grad.astype(LOW), "shard", scatter_dimension=0, tiled=True)


def partners(axis, step):
    return [(i, i ^ step) for i in range(lax.axis_size(axis))]


def steps_of(axis):
    return [1 << bit for bit in range((lax.axis_size(axis) - 1).bit_length())]


def replica_total(grad):
    for step in steps_of("rep"):
        sent = grad.astype(LOW)
        got = lax.ppermute(sent, "rep", partners("rep", step))
        grad = sent.astype(F32) + got.astype(F32)
    return grad


def owner_total(grad):
    me = lax.axis_index("shard")
    count = lax.axis_size("shard")
    rows, columns = grad.shape[0] // count, grad.shape[1]
    left = count
    for step in steps_of("shard"):
        left //= 2
        bit = (me // step) % 2
        pairs = grad.reshape(left, 2, rows, columns)
        mine = lax.dynamic_index_in_dim(pairs, bit, 1, keepdims=False)
        other = lax.dynamic_index_in_dim(pairs, 1 - bit, 1, keepdims=False)
        got = lax.ppermute(other.astype(LOW), "shard", partners("shard", step))
        grad = mine + got.astype(F32)
    return replica_total(grad.reshape(rows, columns))


def sum_everywhere(values):
    for axis in ("shard", "rep"):
        for step in steps_of(axis):
            values = values + lax.ppermute(values, axis, partners(axis, step))
    return values


def on_device(
    tokens,
    seg_ids,
    norm_in_w,
    in_proj,
    conv_w,
    conv_b,
    a_log,
    skip_d,
    dt_bias,
    gnorm_w,
    out_proj,
    cotangent,
):
    length = tokens.shape[0]
    me = lax.axis_index("shard")
    n_in, n_conv, n_gnorm = norm_in_w.shape[0], conv_b.shape[0], gnorm_w.shape[0]
    small = jnp.concatenate([norm_in_w, conv_w.reshape(-1), conv_b, gnorm_w])
    width = in_proj.shape[1] - DIN
    extra = -(-small.shape[0] // width)
    small = jnp.pad(small, (0, extra * width - small.shape[0])).reshape(extra, width)
    joined = lax.all_gather(
        jnp.concatenate([in_proj[:, DIN:], small]), "shard", axis=0, tiled=False
    )
    joined, gate_shard, out_shard = lax.optimization_barrier((joined, in_proj[:, :DIN], out_proj))
    rest_full = joined[:, :n_in].reshape(-1, width)
    small_full = joined[:, n_in:].reshape(joined.shape[0], -1)
    gate_full = lax.all_gather(gate_shard, "shard", axis=0, tiled=True)
    outproj_full = lax.all_gather(out_shard, "shard", axis=0, tiled=True)
    small_full = small_full.astype(F32)
    shards = small_full.shape[0]
    norm_full = small_full[:, :n_in].reshape(-1)
    conv_full = small_full[:, n_in : n_in + DCONV * n_conv]
    conv_full = conv_full.reshape(shards, DCONV, n_conv).transpose(1, 0, 2).reshape(DCONV, -1)
    start = n_in + DCONV * n_conv
    convb_full = small_full[:, start : start + n_conv].reshape(-1)
    start += n_conv
    gnorm_full = small_full[:, start : start + n_gnorm].reshape(-1)

    activation = tokens.astype(F32)
    normed, norm_back = jax.vjp(prenorm, activation, norm_full)
    normed_low = normed.astype(LOW)
    projected = contract_cross(rest_full, normed_low)

    segrow = seg_ids.reshape(-1, BLOCK)
    lasts = segrow[:, BLOCK - 1 :]
    previous = jnp.concatenate([jnp.full((1, 1), -1, lasts.dtype), lasts[:-1]], axis=0)
    keep = (segrow == previous).astype(F32).reshape(1, length)
    tail = (segrow == lasts).astype(F32).reshape(1, length)

    (conv_act, step_size, cumulative), conv_back = jax.vjp(
        lambda *args: conv_and_steps(*args, seg_ids),
        projected[:CONVDIM],
        projected[CONVDIM:],
        conv_full,
        convb_full,
        a_log,
        dt_bias,
    )
    cumcol = cumulative.reshape(GROUPS, GROUP, length).transpose(0, 2, 1)
    operands = (
        conv_act,
        conv_act,
        conv_act,
        step_size.reshape(NH, 1, length),
        cumulative.reshape(NH, 1, length),
        cumcol,
        keep,
        tail,
        seg_ids.reshape(1, length),
        seg_ids.reshape(length, 1),
    )
    scanned, before_states = run_forward(operands, length)
    scanned, gate_full = lax.optimization_barrier((scanned, gate_full))
    gate_part = contract_cross(gate_full, normed_low)
    mixed_out, gate_back = jax.vjp(
        gate_and_norm, scanned, conv_act[:DIN], gate_part, skip_d, gnorm_full
    )
    mixed_low = mixed_out.astype(LOW)
    output = (activation + contract_rows(mixed_low, outproj_full)).astype(LOW)
    grad_out = jnp.dot(mixed_low, cotangent, preferred_element_type=F32)
    grad_out = grad_out.astype(LOW)
    grad_mixed = contract_cols(outproj_full, cotangent)
    gscanned, ghead_skip, ggate, grad_skip, grad_gnorm = gate_back(grad_mixed)
    ggate_low = ggate.astype(LOW)
    grad_gate = contract_cross(normed_low, ggate_low).astype(LOW)
    gscanned, grad_out, grad_gate = lax.optimization_barrier((gscanned, grad_out, grad_gate))
    share_out, share_gate = to_owner(grad_out), to_owner(grad_gate)
    grad_normed = contract_cross(ggate_low, gate_full)

    ghead, gwrite, gread, gstep, gcum, gcumcol = run_backward(
        operands, before_states, gscanned, length
    )
    gcumulative = gcum.reshape(NH, length) - gcumcol.transpose(0, 2, 1).reshape(NH, length)
    gconv_act = jnp.concatenate([ghead + ghead_skip, gwrite, gread], axis=0)
    gconv_in, gstep_raw, grad_conv, grad_convb, grad_alog, grad_step = conv_back(
        (gconv_act, gstep.reshape(NH, length), gcumulative)
    )
    grest_low = jnp.concatenate([gconv_in.astype(LOW), gstep_raw.astype(LOW)], axis=0)
    grest_low, share_out, share_gate = lax.optimization_barrier((grest_low, share_out, share_gate))
    total_out, total_gate = replica_total(share_out), replica_total(share_gate)
    total_rest = owner_total(contract_cross(normed_low, grest_low))
    grad_normed = grad_normed + contract_cross(grest_low, rest_full)
    grad_activation, grad_norm = norm_back(grad_normed)
    grad_tokens = cotangent.astype(F32) + grad_activation

    parts = [grad_norm, grad_conv.reshape(-1), grad_convb, grad_gnorm, grad_alog, grad_skip, grad_step]
    sums = sum_everywhere(jnp.concatenate(parts))
    taken, place = [], 0
    for part in parts:
        taken.append(sums[place : place + part.shape[0]])
        place += part.shape[0]
    own = lambda full, count: lax.dynamic_slice_in_dim(full, me * count, count, axis=-1)
    total_in = jnp.concatenate([total_gate, total_rest], axis=1)
    return (
        output,
        grad_tokens,
        own(taken[0], n_in),
        total_in,
        own(taken[1].reshape(DCONV, -1), n_conv),
        own(taken[2], n_conv),
        taken[4],
        taken[5],
        taken[6],
        own(taken[3], n_gnorm),
        total_out,
    )


def solution(mesh):
    placed = (
        P(("rep", "shard"), None),
        P(("rep", "shard")),
        P("shard"),
        P("shard", None),
        P(None, "shard"),
        P("shard"),
        P(),
        P(),
        P(),
        P("shard"),
        P("shard", None),
        P(("rep", "shard"), None),
    )
    return jax.shard_map(
        on_device,
        mesh=mesh,
        in_specs=placed,
        out_specs=(
            P(("rep", "shard"), None),
            P(("rep", "shard"), None),
            P("shard"),
            P("shard", None),
            P(None, "shard"),
            P("shard"),
            P(),
            P(),
            P(),
            P("shard"),
            P("shard", None),
        ),
        check_vma=False,
    )
```
